32 devices in a mesh: node: 4 (over y, x), feat: 8 (over z, core).
Axes of the slice: x: 2, y: 2, z: 4, core: 2. Of those that a mesh axis runs over, the one named last changes fastest.
Arguments:
- feats: bfloat16 [4096, 256], P(('node', 'feat')), may hold values from -6 to 6
- tile_values: bfloat16 [32, 24, 128, 128], P('node', 'feat'), may hold values from 0.049804688 to 1
- source_group: int32 [32, 24], P('node', 'feat'), may hold values from 0 to 3
- live_slots: int32 [32, 8], P('node', 'feat'), may hold values from 1 to 3, as said below
- proj_weight: bfloat16 [256, 256], replicated, may hold values from -0.375 to 0.375
- proj_bias: float32 [256], replicated, may hold values from -3 to 3
Outputs:
- updated: bfloat16 [4096, 256], P(('node', 'feat'))
The draws below stay inside these ranges and needn't reach their ends.
Inputs may be any that keep to these rules, and one draw needn't show every extreme that they name: `live_slots`: some tile row has all 3 slots live in some column block; slots at or past the count are not part of A.
All inputs are finite; a program needn't handle non-finite values.
Results may differ from the reference program's by a relative error of at most 0.0028.
Values may be sent and summed in bfloat16 or wider, within the bound.
No kernel may reach another device: no remote copies, remote signals or barrier semaphores. Data moves between devices by JAX's collectives and lax.ppermute only.
A program may use at most 64 MiB of HBM per device.

```python
import math
import jax
import jax.numpy as jnp
import numpy as np
from jax import lax

FEATURES = 256
TILE = 128
SLOTS = 3
NODE_BLOCKS = 4
COLBLOCKS = 8
GROUPS = 32
NODES = 4096


def draw_live_slots(key, part):
    column_index = jnp.arange(COLBLOCKS, dtype=jnp.int32)[None, :]
    spread_last = max(COLBLOCKS - 1, 1)
    ceiling = 1 + (SLOTS - 1) * column_index // spread_last
    raw_draw = jax.random.randint(key, (GROUPS, COLBLOCKS), 0, 1 << 20, dtype=jnp.int32)
    drawn = 1 + raw_draw % ceiling
    leading = jnp.arange(GROUPS, dtype=jnp.int32)[:, None] % COLBLOCKS == 0
    return jnp.where(leading, ceiling, drawn).astype(jnp.int32)


def plant(entries, rng, smallest, largest):
    longest = entries.shape.index(max(entries.shape))
    spots = []
    for shift in (0, 1):
        where = [jax.random.randint(jax.random.fold_in(rng, axis), (), 0, length) for axis, length in enumerate(entries.shape)]
        where[longest] = (where[longest] + shift) % entries.shape[longest]
        spots.append(tuple(where))
    return entries.at[spots[0]].set(smallest).at[spots[1]].set(largest)


def shard_levels(rng, dims, split, low, high):
    def one(position, blocks):
        steps = jax.random.uniform(jax.random.fold_in(jax.random.fold_in(rng, 6), position), (blocks,), jnp.float32, low / len(split), high / len(split))
        return jnp.repeat(jnp.exp(steps), dims[position] // blocks).reshape((-1,) + (1,) * (len(dims) - position - 1))

    factor_of = one(*split[0])
    for cut in split[1:]:
        factor_of = factor_of * one(*cut)
    return factor_of


def rank_bounds(number_of, slope):
    loads = [(1 << 20) // math.isqrt(rank ** slope) + 1 for rank in range(1, number_of + 1)]
    width = 1 + sum(loads) // (1 << 30)
    return np.cumsum(np.array([max(1, weight // width) for weight in loads]))


def skewed_ids(stream_key, extent, amount, lean):
    table = rank_bounds(amount, lean)
    pick = jax.random.randint(jax.random.fold_in(stream_key, 1), extent, 0, int(table[amount - 1]))
    rank = jnp.searchsorted(jnp.asarray(table, jnp.int32), pick, side="right")
    return jax.random.permutation(jax.random.fold_in(stream_key, 2), amount)[rank].astype(jnp.int32)


def normal_values(key, shape, width, reach, split=(), held_as=jnp.bfloat16):
    array = width * jax.random.normal(key, shape, jnp.float32)
    if split:
        array = array * shard_levels(key, shape, split, -0.22, 0.18)
    return jnp.clip(array, -reach, reach).astype(held_as)


def setup_inputs(seed: int = 0) -> dict:
    key_of = jax.random.split(jax.random.key(seed), 7)
    return {
        "feats": normal_values(key_of[0], (NODES, FEATURES), 1.0, 6.0, ((0, 32),)),
        "tile_values": jnp.clip(0.049804688 + 0.9501953 * jax.random.uniform(key_of[1], (GROUPS, COLBLOCKS * SLOTS, TILE, TILE), jnp.float32) ** shard_levels(key_of[1], (GROUPS, COLBLOCKS * SLOTS, TILE, TILE), ((0, 4), (1, 8)), -0.2, 0.2), 0.049804688, 1.0).astype(jnp.bfloat16),
        "source_group": plant(skewed_ids(key_of[2], (GROUPS, COLBLOCKS * SLOTS), NODE_BLOCKS, 2), jax.random.fold_in(key_of[2], 3), 0, NODE_BLOCKS - 1).astype(jnp.int32),
        "live_slots": draw_live_slots(jax.random.fold_in(key_of[6], 71), 0),
        "proj_weight": normal_values(key_of[4], (FEATURES, FEATURES), FEATURES ** -0.5, 0.375),
        "proj_bias": normal_values(key_of[5], (FEATURES,), 0.5, 3.0, (), jnp.float32),
    }


def reference(feats, tile_values, source_group, live_slots, proj_weight, proj_bias):
    source_rows = feats.reshape(GROUPS, TILE, FEATURES)
    column_of = jnp.arange(COLBLOCKS * SLOTS, dtype=jnp.int32) // SLOTS
    slot_of = jnp.arange(COLBLOCKS * SLOTS, dtype=jnp.int32) % SLOTS

    def one_group(group_args):
        tiles, sources, live_row = group_args
        keep_slot = slot_of < live_row[column_of]
        adjacency = tiles.astype(jnp.float32)
        adjacency = jnp.where(keep_slot[:, None, None], adjacency, jnp.zeros_like(adjacency))
        gathered = source_rows[(sources * COLBLOCKS + column_of).astype(jnp.int32)].astype(jnp.float32)
        aggregate = jnp.einsum('sab,sbf->af', adjacency, gathered)
        degree_sum = 1.0 + lax.optimization_barrier(jnp.sum(adjacency, axis=(0, 2)))
        return (aggregate, degree_sum)
    aggregate, degree_sum = lax.map(one_group, (tile_values, source_group, live_slots))
    aggregate = aggregate.reshape(NODES, FEATURES)
    degree_sum = degree_sum.reshape(NODES)
    own_rows = feats.astype(jnp.float32)
    normed = ((aggregate + own_rows) * lax.rsqrt(degree_sum)[:, None]).astype(jnp.bfloat16)
    hidden = jnp.dot(normed, proj_weight, preferred_element_type=jnp.float32) + proj_bias.astype(jnp.float32)
    return (own_rows + jax.nn.relu(hidden)).astype(jnp.bfloat16)
```

```python
import functools

import jax
import jax.numpy as jnp
from jax import lax
from jax.experimental import pallas as pl
from jax.experimental.pallas import tpu as pltpu
from jax.sharding import PartitionSpec as P

EXTRA = 16
VMEM = pl.BlockSpec(memory_space=pltpu.VMEM)
SMEM = pl.BlockSpec(memory_space=pltpu.SMEM)
ANY = pl.BlockSpec(memory_space=pl.ANY)
PARAMS = pltpu.CompilerParams(vmem_limit_bytes=32 * 1024 * 1024)


def partner(index, step, count):
    if count & (count - 1) == 0:
        return index ^ step
    return (index + step) % count


def partner_back(index, step, count):
    if count & (count - 1) == 0:
        return index ^ step
    return (index + count - step) % count


def split_rows(degree):
    high = degree.astype(jnp.bfloat16)
    low = (degree - high.astype(jnp.float32)).astype(jnp.bfloat16)
    return jnp.concatenate([high, low], axis=1)


def join_rows(rows):
    rows = rows.astype(jnp.float32)
    half = rows.shape[1] // 2
    return rows[:, :half] + rows[:, half:]


def prepare_kernel(live, tiles, adjacency, degree):
    groups, slots, tile, _ = tiles.shape
    ones = jnp.ones((EXTRA, slots * tile), jnp.bfloat16)
    for group in range(groups):
        count = live[group, 0]
        wide = []
        for slot in range(slots):
            block = tiles[group, slot]
            wide.append(jnp.where(slot < count, block, jnp.zeros_like(block)))
        wide = jnp.concatenate(wide, axis=1)
        adjacency[group] = wide
        degree[group] = lax.dot_general(
            ones, wide, (((1,), (1,)), ((), ())), preferred_element_type=jnp.float32
        )


def aggregate_kernel(nodes, chips, slots, mine, *refs):
    src, adjacency, degree = refs[:3]
    feats_in = refs[3 : 3 + nodes]
    out, rows = refs[3 + nodes :]
    node = lax.axis_index("node")
    feat = lax.axis_index("feat")
    chip = feat // 2
    core = feat % 2 if mine else 1 - feat % 2
    tile = feats_in[0].shape[0]
    for step in range(nodes):
        rows[partner_back(node, step, nodes)] = feats_in[step][...]
    for step in range(chips):
        group = partner(chip, step, chips) * 2 + core
        right = jnp.concatenate([rows[src[group, slot]] for slot in range(slots)], axis=0)
        product = jnp.dot(adjacency[group], right, preferred_element_type=jnp.float32)
        out[step, :tile] = product.astype(out.dtype)
        out[step, tile:] = split_rows(degree[group]).astype(out.dtype)


def merge_kernel(mine, theirs, own, *outs):
    tile = mine.shape[1] - EXTRA
    for step in range(mine.shape[0]):
        total = mine[step, :tile] + theirs[step, :tile].astype(jnp.float32)
        degree = split_rows(join_rows(mine[step, tile:]) + join_rows(theirs[step, tile:]))
        out = outs[step - 1] if step else own
        out[:tile] = total.astype(out.dtype)
        out[tile:] = degree.astype(out.dtype)


def update_kernel(*refs):
    own, *parts, feats, weight, bias, out = refs
    tile = feats.shape[0]
    total = own[...]
    for part in parts:
        total = total + part[...].astype(jnp.float32)
    degree = join_rows(total[tile:])[:1]
    scale = jnp.transpose(jnp.broadcast_to(lax.rsqrt(degree + 1.0), (tile, tile)))
    scale = jnp.concatenate([scale] * (feats.shape[1] // tile), axis=1)
    rows = feats[...].astype(jnp.float32)
    normed = ((total[:tile] + rows) * scale).astype(jnp.bfloat16)
    hidden = jnp.dot(normed, weight[...], preferred_element_type=jnp.float32) + bias[...]
    out[...] = (rows + jnp.maximum(hidden, 0.0)).astype(jnp.bfloat16)


def body(mesh, feats, tile_values, source_group, live_slots, proj_weight, proj_bias):
    nodes, chips = mesh.shape["node"], mesh.shape["feat"] // 2
    groups, slots = tile_values.shape[:2]
    tile, width = feats.shape

    def over_nodes(step):
        pairs = [(n, partner(n, step, nodes)) for n in range(nodes)]
        return lax.ppermute(feats, "node", pairs)

    def over_chips(array, step):
        pairs = [(2 * z + c, 2 * partner(z, step, chips) + c) for z in range(chips) for c in range(2)]
        return lax.ppermute(array, "feat", pairs)

    def over_cores(array):
        return lax.ppermute(array, "feat", [(f, f ^ 1) for f in range(2 * chips)])

    rows_in = [feats] + [over_nodes(step) for step in range(1, nodes)]
    adjacency, degree = pl.pallas_call(
        prepare_kernel,
        out_shape=[
            jax.ShapeDtypeStruct((groups, tile, slots * tile), jnp.bfloat16),
            jax.ShapeDtypeStruct((groups, EXTRA, tile), jnp.float32),
        ],
        in_specs=[SMEM, VMEM],
        out_specs=[VMEM, VMEM],
        compiler_params=PARAMS,
        cost_estimate=pl.CostEstimate(flops=1 << 27, bytes_accessed=1 << 22, transcendentals=0),
    )(live_slots, tile_values)

    def aggregate(mine):
        dtype = jnp.float32 if mine else jnp.bfloat16
        return pl.pallas_call(
            functools.partial(aggregate_kernel, nodes, chips, slots, mine),
            out_shape=jax.ShapeDtypeStruct((chips, tile + EXTRA, width), dtype),
            in_specs=[SMEM] + [VMEM] * (2 + nodes),
            out_specs=VMEM,
            scratch_shapes=[pltpu.VMEM((nodes, tile, width), jnp.bfloat16)],
            compiler_params=PARAMS,
            cost_estimate=pl.CostEstimate(flops=1 << 27, bytes_accessed=1 << 22, transcendentals=0),
        )(source_group, adjacency, degree, *rows_in)

    theirs = over_cores(aggregate(False))
    own, *parts = pl.pallas_call(
        merge_kernel,
        out_shape=[jax.ShapeDtypeStruct((tile + EXTRA, width), jnp.float32)]
        + [jax.ShapeDtypeStruct((tile + EXTRA, width), jnp.bfloat16)] * (chips - 1),
        in_specs=[VMEM] * 2,
        out_specs=[VMEM] * chips,
        compiler_params=PARAMS,
    )(aggregate(True), theirs)
    parts = [over_chips(part, step) for step, part in enumerate(parts, 1)]
    return pl.pallas_call(
        update_kernel,
        out_shape=jax.ShapeDtypeStruct((tile, width), jnp.bfloat16),
        in_specs=[VMEM] * (chips + 3),
        out_specs=VMEM,
        compiler_params=PARAMS,
    )(own, *parts, feats, proj_weight, proj_bias.reshape(1, -1))


def solution(mesh):
    placed = (
        P(("node", "feat"), None),
        P("node", "feat", None, None),
        P("node", "feat"),
        P("node", "feat"),
        P(),
        P(),
    )
    return jax.shard_map(
        functools.partial(body, mesh),
        mesh=mesh,
        in_specs=placed,
        out_specs=P(("node", "feat"), None),
        check_vma=False,
    )
```

```python
import functools

import jax
import jax.numpy as jnp
from jax import lax
from jax.experimental import pallas as pl
from jax.experimental.pallas import tpu as pltpu
from jax.sharding import PartitionSpec as P

EXTRA = 16
VMEM = pl.BlockSpec(memory_space=pltpu.VMEM)
SMEM = pl.BlockSpec(memory_space=pltpu.SMEM)
HBM = pl.BlockSpec(memory_space=pltpu.HBM)
PARAMS = pltpu.CompilerParams(vmem_limit_bytes=32 * 1024 * 1024)


def partner(index, step, count):
    if count & (count - 1) == 0:
        return index ^ step
    return (index + step) % count


def partner_back(index, step, count):
    if count & (count - 1) == 0:
        return index ^ step
    return (index + count - step) % count


def along_line(chip, step, chips):
    odd = chip % 2
    place = odd * (chips - 1) + (1 - 2 * odd) * (chip // 2)
    place = (place + chips - step) % chips
    back = place // ((chips + 1) // 2)
    return back * (2 * (chips - 1 - place) + 1) + (1 - back) * 2 * place


def split_rows(degree):
    high = degree.astype(jnp.bfloat16)
    low = (degree - high.astype(jnp.float32)).astype(jnp.bfloat16)
    return jnp.concatenate([high, low], axis=1)


def join_rows(rows):
    rows = rows.astype(jnp.float32)
    half = rows.shape[1] // 2
    return rows[:, :half] + rows[:, half:]


def group_order(chips):
    chip, core = lax.axis_index("feat") // 2, lax.axis_index("feat") % 2
    return [
        along_line(chip, step, chips) * 2 + (core if mine else 1 - core)
        for mine in range(2)
        for step in range(chips)
    ]


def prepare_kernel(
    live_in, src_in, tiles_in, feats_in, weight_in, bias_in,
    adjacency, degree, chosen, feats, weight, bias,
    live, src, tiles, tile_sems, sems,
):
    groups, slots, tile, _ = tiles.shape
    order = group_order(groups // 2)
    small = [
        pltpu.make_async_copy(live_in, live, sems.at[0]),
        pltpu.make_async_copy(src_in, src, sems.at[1]),
        pltpu.make_async_copy(feats_in, feats, sems.at[2]),
        pltpu.make_async_copy(weight_in, weight, sems.at[3]),
        pltpu.make_async_copy(bias_in, bias, sems.at[4]),
    ]
    large = [
        pltpu.make_async_copy(tiles_in.at[group], tiles.at[place], tile_sems.at[place])
        for place, group in enumerate(order)
    ]
    small[0].start()
    small[1].start()
    for copy in large:
        copy.start()
    for copy in small[2:]:
        copy.start()
    ones = jnp.ones((EXTRA, slots * tile), jnp.bfloat16)
    small[0].wait()
    small[1].wait()
    for place, group in enumerate(order):
        for slot in range(slots):
            row = place * slots + slot
            chosen[row : row + 1] = jnp.full((1, chosen.shape[1]), src[slot, group], jnp.int32)
    for place, group in enumerate(order):
        large[place].wait()
        count = live[0, group]
        wide = []
        for slot in range(slots):
            block = tiles[place, slot]
            wide.append(jnp.where(slot < count, block, jnp.zeros_like(block)))
        wide = jnp.concatenate(wide, axis=1)
        adjacency[place] = wide
        degree[place] = lax.dot_general(
            ones, wide, (((1,), (1,)), ((), ())), preferred_element_type=jnp.float32
        )
    for copy in small[2:]:
        copy.wait()


def aggregate_kernel(nodes, chips, slots, mine, *refs):
    chosen, adjacency, degree = refs[:3]
    feats_in = refs[3 : 3 + nodes]
    out, rows = refs[3 + nodes :]
    node = lax.axis_index("node")
    tile = feats_in[0].shape[0]
    for step in range(nodes):
        rows[partner_back(node, step, nodes)] = feats_in[step][...]
    for step in range(chips):
        place = mine * chips + step
        picks = [chosen[place * slots + slot, 0] for slot in range(slots)]
        right = jnp.concatenate([rows[pick] for pick in picks], axis=0)
        product = jnp.dot(adjacency[place], right, preferred_element_type=jnp.float32)
        out[step, :tile] = product.astype(out.dtype)
        out[step, tile:] = split_rows(degree[place]).astype(out.dtype)


def merge_kernel(mine, theirs, own, *outs):
    tile = mine.shape[1] - EXTRA
    for step in range(mine.shape[0]):
        total = mine[step, :tile] + theirs[step, :tile].astype(jnp.float32)
        degree = split_rows(join_rows(mine[step, tile:]) + join_rows(theirs[step, tile:]))
        out = outs[step - 1] if step else own
        out[:tile] = total.astype(out.dtype)
        out[tile:] = degree.astype(out.dtype)


def update_kernel(*refs):
    own, *parts, feats, weight, bias, out = refs
    tile = feats.shape[0]
    total = own[...]
    for part in parts:
        total = total + part[...].astype(jnp.float32)
    degree = join_rows(total[tile:])[:1]
    scale = jnp.transpose(jnp.broadcast_to(lax.rsqrt(degree + 1.0), (tile, tile)))
    scale = jnp.concatenate([scale] * (feats.shape[1] // tile), axis=1)
    rows = feats[...].astype(jnp.float32)
    normed = ((total[:tile] + rows) * scale).astype(jnp.bfloat16)
    hidden = jnp.dot(normed, weight[...], preferred_element_type=jnp.float32) + bias[...]
    out[...] = (rows + jnp.maximum(hidden, 0.0)).astype(jnp.bfloat16)


def body(mesh, feats, tile_values, source_group, live_slots, proj_weight, proj_bias):
    nodes, chips = mesh.shape["node"], mesh.shape["feat"] // 2
    groups, slots = tile_values.shape[:2]
    live_slots, source_group = live_slots.T, source_group.T
    tile, width = feats.shape

    def over_nodes(step):
        pairs = [(n, partner(n, step, nodes)) for n in range(nodes)]
        return lax.ppermute(feats, "node", pairs)

    def over_chips(array, step):
        pairs = [(2 * z + c, 2 * along_line(z, step, chips) + c) for z in range(chips) for c in range(2)]
        return lax.ppermute(array, "feat", pairs)

    def over_cores(array):
        return lax.ppermute(array, "feat", [(f, f ^ 1) for f in range(2 * chips)])

    rows_in = [over_nodes(step) for step in range(1, nodes)]
    adjacency, degree, chosen, own_feats, weight, bias = pl.pallas_call(
        prepare_kernel,
        out_shape=[
            jax.ShapeDtypeStruct((groups, tile, slots * tile), jnp.bfloat16),
            jax.ShapeDtypeStruct((groups, EXTRA, tile), jnp.float32),
            jax.ShapeDtypeStruct((groups * slots, 128), jnp.int32),
            jax.ShapeDtypeStruct(feats.shape, feats.dtype),
            jax.ShapeDtypeStruct(proj_weight.shape, proj_weight.dtype),
            jax.ShapeDtypeStruct((1, width), proj_bias.dtype),
        ],
        in_specs=[HBM] * 6,
        out_specs=[VMEM] * 6,
        scratch_shapes=[
            pltpu.SMEM(live_slots.shape, live_slots.dtype),
            pltpu.SMEM(source_group.shape, source_group.dtype),
            pltpu.VMEM(tile_values.shape, tile_values.dtype),
            pltpu.SemaphoreType.DMA((groups,)),
            pltpu.SemaphoreType.DMA((5,)),
        ],
        compiler_params=PARAMS,
        cost_estimate=pl.CostEstimate(flops=1 << 27, bytes_accessed=1 << 22, transcendentals=0),
    )(
        *(
            pltpu.with_memory_space_constraint(array, pltpu.HBM)
            for array in (live_slots, source_group, tile_values, feats, proj_weight, proj_bias.reshape(1, -1))
        )
    )
    rows_in = [own_feats] + rows_in

    def aggregate(mine):
        dtype = jnp.float32 if mine else jnp.bfloat16
        return pl.pallas_call(
            functools.partial(aggregate_kernel, nodes, chips, slots, mine),
            out_shape=jax.ShapeDtypeStruct((chips, tile + EXTRA, width), dtype),
            in_specs=[VMEM] * (3 + nodes),
            out_specs=VMEM,
            scratch_shapes=[pltpu.VMEM((nodes, tile, width), jnp.bfloat16)],
            compiler_params=PARAMS,
            cost_estimate=pl.CostEstimate(flops=1 << 27, bytes_accessed=1 << 22, transcendentals=0),
        )(chosen, adjacency, degree, *rows_in)

    theirs = over_cores(aggregate(False))
    own, *parts = pl.pallas_call(
        merge_kernel,
        out_shape=[jax.ShapeDtypeStruct((tile + EXTRA, width), jnp.float32)]
        + [jax.ShapeDtypeStruct((tile + EXTRA, width), jnp.bfloat16)] * (chips - 1),
        in_specs=[VMEM] * 2,
        out_specs=[VMEM] * chips,
        compiler_params=PARAMS,
    )(aggregate(True), theirs)
    parts = [over_chips(part, step) for step, part in enumerate(parts, 1)]
    return pl.pallas_call(
        update_kernel,
        out_shape=jax.ShapeDtypeStruct((tile, width), jnp.bfloat16),
        in_specs=[VMEM] * (chips + 3),
        out_specs=VMEM,
        compiler_params=PARAMS,
    )(own, *parts, own_feats, weight, bias)


def solution(mesh):
    placed = (
        P(("node", "feat"), None),
        P("node", "feat", None, None),
        P("node", "feat"),
        P("node", "feat"),
        P(),
        P(),
    )
    return jax.shard_map(
        functools.partial(body, mesh),
        mesh=mesh,
        in_specs=placed,
        out_specs=P(("node", "feat"), None),
        check_vma=False,
    )
```

```python
import functools

import jax
import jax.numpy as jnp
from jax import lax
from jax.experimental import pallas as pl
from jax.experimental.pallas import tpu as pltpu
from jax.sharding import PartitionSpec as P

EXTRA = 8
FIRST = 2
VMEM = pl.BlockSpec(memory_space=pltpu.VMEM)
SMEM = pl.BlockSpec(memory_space=pltpu.SMEM)
HBM = pl.BlockSpec(memory_space=pltpu.HBM)
PARAMS = pltpu.CompilerParams(vmem_limit_bytes=32 * 1024 * 1024)


def along_ring(index, step, count):
    odd = index % 2
    place = odd * (count - 1) + (1 - 2 * odd) * (index // 2)
    place = (place + count - step) % count
    back = place // ((count + 1) // 2)
    return back * (2 * (count - 1 - place) + 1) + (1 - back) * 2 * place


def split_rows(degree):
    high = degree.astype(jnp.bfloat16)
    low = (degree - high.astype(jnp.float32)).astype(jnp.bfloat16)
    return jnp.concatenate([high, low], axis=1)


def join_rows(rows):
    rows = rows.astype(jnp.float32)
    half = rows.shape[1] // 2
    return rows[:, :half] + rows[:, half:]


def group_order(chips):
    chip, core = lax.axis_index("feat") // 2, lax.axis_index("feat") % 2
    return [
        along_ring(chip, step, chips) * 2 + (core if mine else 1 - core)
        for mine in range(2)
        for step in range(chips)
    ]


def prepare_kernel(
    live_in, src_in, tiles_in, feats_in, weight_in, bias_in,
    adjacency, degree, chosen, feats, weight, bias,
    live, src, tiles, tile_sems, sems,
):
    groups, slots, tile, _ = tiles.shape
    order = group_order(groups // 2)
    small = [
        pltpu.make_async_copy(live_in, live, sems.at[0]),
        pltpu.make_async_copy(src_in, src, sems.at[1]),
        pltpu.make_async_copy(feats_in, feats, sems.at[2]),
        pltpu.make_async_copy(weight_in, weight, sems.at[3]),
        pltpu.make_async_copy(bias_in, bias, sems.at[4]),
    ]
    large = [
        pltpu.make_async_copy(tiles_in.at[group], tiles.at[place], tile_sems.at[place])
        for place, group in enumerate(order)
    ]
    small[0].start()
    small[1].start()
    for copy in large:
        copy.start()
    for copy in small[2:]:
        copy.start()
    ones = jnp.ones((EXTRA, slots * tile), jnp.bfloat16)
    small[0].wait()
    small[1].wait()
    for place, group in enumerate(order):
        for slot in range(slots):
            row = place * slots + slot
            chosen[row : row + 1] = jnp.full((1, chosen.shape[1]), src[slot, group], jnp.int32)
    for place, group in enumerate(order):
        large[place].wait()
        count = live[0, group]
        wide = []
        for slot in range(slots):
            block = tiles[place, slot]
            wide.append(jnp.where(slot < count, block, jnp.zeros_like(block)))
        wide = jnp.concatenate(wide, axis=1)
        adjacency[place] = wide
        degree[place] = lax.dot_general(
            ones, wide, (((1,), (1,)), ((), ())), preferred_element_type=jnp.float32
        )
    for copy in small[2:]:
        copy.wait()


def aggregate_kernel(nodes, chips, slots, mine, steps, *refs):
    chosen, adjacency, degree = refs[:3]
    feats_in = refs[3 : 3 + nodes]
    out, rows = refs[3 + nodes :]
    node = lax.axis_index("node")
    tile = feats_in[0].shape[0]
    for step in range(nodes):
        rows[along_ring(node, (nodes - step) % nodes, nodes)] = feats_in[step][...]
    for index, step in enumerate(steps):
        place = mine * chips + step
        picks = [chosen[place * slots + slot, 0] for slot in range(slots)]
        right = jnp.concatenate([rows[pick] for pick in picks], axis=0)
        product = jnp.dot(adjacency[place], right, preferred_element_type=jnp.float32)
        out[index, :tile] = product.astype(out.dtype)
        out[index, tile:] = split_rows(degree[place]).astype(out.dtype)


def merge_kernel(mine, theirs, *outs):
    tile = mine.shape[1] - EXTRA
    for index, out in enumerate(outs):
        total = mine[index, :tile] + theirs[index, :tile].astype(jnp.float32)
        degree = split_rows(join_rows(mine[index, tile:]) + join_rows(theirs[index, tile:]))
        out[:tile] = total.astype(out.dtype)
        out[tile:] = degree.astype(out.dtype)


def update_kernel(*refs):
    own, *parts, feats, weight, bias, out = refs
    tile = feats.shape[0]
    total = own[...]
    for part in parts:
        total = total + part[...].astype(jnp.float32)
    degree = join_rows(total[tile:])[:1]
    scale = jnp.transpose(jnp.broadcast_to(lax.rsqrt(degree + 1.0), (tile, tile)))
    scale = jnp.concatenate([scale] * (feats.shape[1] // tile), axis=1)
    rows = feats[...].astype(jnp.float32)
    normed = ((total[:tile] + rows) * scale).astype(jnp.bfloat16)
    hidden = jnp.dot(normed, weight[...], preferred_element_type=jnp.float32) + bias[...]
    out[...] = (rows + jnp.maximum(hidden, 0.0)).astype(jnp.bfloat16)


def body(mesh, feats, tile_values, source_group, live_slots, proj_weight, proj_bias):
    nodes, chips = mesh.shape["node"], mesh.shape["feat"] // 2
    groups, slots = tile_values.shape[:2]
    live_slots, source_group = live_slots.T, source_group.T
    tile, width = feats.shape

    def over_nodes(step):
        pairs = [(n, along_ring(n, step, nodes)) for n in range(nodes)]
        return lax.ppermute(feats, "node", pairs)

    def over_chips(array, step):
        pairs = [(2 * z + c, 2 * along_ring(z, step, chips) + c) for z in range(chips) for c in range(2)]
        return lax.ppermute(array, "feat", pairs)

    def over_cores(array):
        return lax.ppermute(array, "feat", [(f, f ^ 1) for f in range(2 * chips)])

    rows_in = [over_nodes(step) for step in range(1, nodes)]
    adjacency, degree, chosen, own_feats, weight, bias = pl.pallas_call(
        prepare_kernel,
        out_shape=[
            jax.ShapeDtypeStruct((groups, tile, slots * tile), jnp.bfloat16),
            jax.ShapeDtypeStruct((groups, EXTRA, tile), jnp.float32),
            jax.ShapeDtypeStruct((groups * slots, 128), jnp.int32),
            jax.ShapeDtypeStruct(feats.shape, feats.dtype),
            jax.ShapeDtypeStruct(proj_weight.shape, proj_weight.dtype),
            jax.ShapeDtypeStruct((1, width), proj_bias.dtype),
        ],
        in_specs=[HBM] * 6,
        out_specs=[VMEM] * 6,
        scratch_shapes=[
            pltpu.SMEM(live_slots.shape, live_slots.dtype),
            pltpu.SMEM(source_group.shape, source_group.dtype),
            pltpu.VMEM(tile_values.shape, tile_values.dtype),
            pltpu.SemaphoreType.DMA((groups,)),
            pltpu.SemaphoreType.DMA((5,)),
        ],
        compiler_params=PARAMS,
        cost_estimate=pl.CostEstimate(flops=1 << 27, bytes_accessed=1 << 22, transcendentals=0),
    )(
        *(
            pltpu.with_memory_space_constraint(array, pltpu.HBM)
            for array in (live_slots, source_group, tile_values, feats, proj_weight, proj_bias.reshape(1, -1))
        )
    )
    rows_in = [own_feats] + rows_in

    def aggregate(mine, steps):
        dtype = jnp.float32 if mine else jnp.bfloat16
        return pl.pallas_call(
            functools.partial(aggregate_kernel, nodes, chips, slots, mine, steps),
            out_shape=jax.ShapeDtypeStruct((len(steps), tile + EXTRA, width), dtype),
            in_specs=[VMEM] * (3 + nodes),
            out_specs=VMEM,
            scratch_shapes=[pltpu.VMEM((nodes, tile, width), jnp.bfloat16)],
            compiler_params=PARAMS,
            cost_estimate=pl.CostEstimate(flops=1 << 27, bytes_accessed=1 << 22, transcendentals=0),
        )(chosen, adjacency, degree, *rows_in)

    def merge(mine, theirs, dtypes):
        return pl.pallas_call(
            merge_kernel,
            out_shape=[jax.ShapeDtypeStruct((tile + EXTRA, width), dtype) for dtype in dtypes],
            in_specs=[VMEM] * 2,
            out_specs=[VMEM] * len(dtypes),
            compiler_params=PARAMS,
        )(mine, theirs)

    cut = min(chips, FIRST + 1)
    far, near = list(range(1, cut)), list(range(cut, chips)) + [0]
    theirs_far = over_cores(aggregate(0, far))
    theirs_near = over_cores(aggregate(0, near))
    parts = merge(aggregate(1, far), theirs_far, [jnp.bfloat16] * len(far))
    *rest, own = merge(aggregate(1, near), theirs_near, [jnp.bfloat16] * (len(near) - 1) + [jnp.float32])
    parts = [over_chips(part, step) for step, part in enumerate([*parts, *rest], 1)]
    return pl.pallas_call(
        update_kernel,
        out_shape=jax.ShapeDtypeStruct((tile, width), jnp.bfloat16),
        in_specs=[VMEM] * (chips + 3),
        out_specs=VMEM,
        compiler_params=PARAMS,
    )(own, *parts, own_feats, weight, bias)


def solution(mesh):
    placed = (
        P(("node", "feat"), None),
        P("node", "feat", None, None),
        P("node", "feat"),
        P("node", "feat"),
        P(),
        P(),
    )
    return jax.shard_map(
        functools.partial(body, mesh),
        mesh=mesh,
        in_specs=placed,
        out_specs=P(("node", "feat"), None),
        check_vma=False,
    )
```

```python
import functools

import jax
import jax.numpy as jnp
from jax import lax
from jax.experimental import pallas as pl
from jax.experimental.pallas import tpu as pltpu
from jax.sharding import PartitionSpec as P

EXTRA = 8
FIRST = 2
VMEM = pl.BlockSpec(memory_space=pltpu.VMEM)
SMEM = pl.BlockSpec(memory_space=pltpu.SMEM)
HBM = pl.BlockSpec(memory_space=pltpu.HBM)
PARAMS = pltpu.CompilerParams(vmem_limit_bytes=32 * 1024 * 1024)


def along_ring(index, step, count):
    odd = index % 2
    place = odd * (count - 1) + (1 - 2 * odd) * (index // 2)
    place = (place + count - step) % count
    back = place // ((count + 1) // 2)
    return back * (2 * (count - 1 - place) + 1) + (1 - back) * 2 * place


def split_rows(degree):
    high = degree.astype(jnp.bfloat16)
    low = (degree - high.astype(jnp.float32)).astype(jnp.bfloat16)
    return jnp.concatenate([high, low], axis=1)


def join_rows(rows):
    rows = rows.astype(jnp.float32)
    half = rows.shape[1] // 2
    return rows[:, :half] + rows[:, half:]


def group_order(chips):
    chip, core = lax.axis_index("feat") // 2, lax.axis_index("feat") % 2
    return [
        along_ring(chip, step, chips) * 2 + (core if mine else 1 - core)
        for mine in range(2)
        for step in range(chips)
    ]


def prepare_kernel(
    live_in, src_in, tiles_in, feats_in, weight_in, bias_in,
    adjacency, degree, chosen, feats, weight, bias,
    live, src, tiles, tile_sems, sems,
):
    groups, slots, tile, _ = tiles.shape
    order = group_order(groups // 2)
    small = [
        pltpu.make_async_copy(live_in, live, sems.at[0]),
        pltpu.make_async_copy(src_in, src, sems.at[1]),
        pltpu.make_async_copy(feats_in, feats, sems.at[2]),
        pltpu.make_async_copy(weight_in, weight, sems.at[3]),
        pltpu.make_async_copy(bias_in, bias, sems.at[4]),
    ]
    large = [
        pltpu.make_async_copy(tiles_in.at[group], tiles.at[place], tile_sems.at[place])
        for place, group in enumerate(order)
    ]
    small[0].start()
    small[1].start()
    for copy in large:
        copy.start()
    for copy in small[2:]:
        copy.start()
    ones = jnp.ones((EXTRA, slots * tile), jnp.bfloat16)
    small[0].wait()
    small[1].wait()
    for place, group in enumerate(order):
        for slot in range(slots):
            row = place * slots + slot
            chosen[row : row + 1] = jnp.full((1, chosen.shape[1]), src[slot, group], jnp.int32)
    for place, group in enumerate(order):
        large[place].wait()
        count = live[0, group]
        wide = []
        for slot in range(slots):
            block = tiles[place, slot]
            wide.append(jnp.where(slot < count, block, jnp.zeros_like(block)))
        wide = jnp.concatenate(wide, axis=1)
        adjacency[place] = wide
        degree[place] = lax.dot_general(
            ones, wide, (((1,), (1,)), ((), ())), preferred_element_type=jnp.float32
        )
    for copy in small[2:]:
        copy.wait()


def aggregate_kernel(nodes, chips, slots, mine, steps, *refs):
    chosen, adjacency, degree = refs[:3]
    feats_in = refs[3 : 3 + nodes]
    out, rows = refs[3 + nodes :]
    node = lax.axis_index("node")
    tile = feats_in[0].shape[0]
    for step in range(nodes):
        rows[along_ring(node, (nodes - step) % nodes, nodes)] = feats_in[step][...]
    for index, step in enumerate(steps):
        place = mine * chips + step
        picks = [chosen[place * slots + slot, 0] for slot in range(slots)]
        right = jnp.concatenate([rows[pick] for pick in picks], axis=0)
        product = jnp.dot(adjacency[place], right, preferred_element_type=jnp.float32)
        out[index, :tile] = product.astype(out.dtype)
        out[index, tile:] = split_rows(degree[place]).astype(out.dtype)


def merge_kernel(mine, theirs, *outs):
    tile = mine.shape[1] - EXTRA
    for index, out in enumerate(outs):
        total = mine[index, :tile] + theirs[index, :tile].astype(jnp.float32)
        degree = split_rows(join_rows(mine[index, tile:]) + join_rows(theirs[index, tile:]))
        out[:tile] = total.astype(out.dtype)
        out[tile:] = degree.astype(out.dtype)


def update_kernel(*refs):
    own, *parts, feats, weight, bias, out = refs
    tile = feats.shape[0]
    total = own[...]
    for part in parts:
        total = total + part[...].astype(jnp.float32)
    degree = join_rows(total[tile:])[:1]
    scale = jnp.transpose(jnp.broadcast_to(lax.rsqrt(degree + 1.0), (tile, tile)))
    scale = jnp.concatenate([scale] * (feats.shape[1] // tile), axis=1)
    rows = feats[...].astype(jnp.float32)
    normed = ((total[:tile] + rows) * scale).astype(jnp.bfloat16)
    hidden = jnp.dot(normed, weight[...], preferred_element_type=jnp.float32) + bias[...]
    out[...] = (rows + jnp.maximum(hidden, 0.0)).astype(jnp.bfloat16)


def body(mesh, feats, tile_values, source_group, live_slots, proj_weight, proj_bias):
    nodes, chips = mesh.shape["node"], mesh.shape["feat"] // 2
    groups, slots = tile_values.shape[:2]
    live_slots, source_group = live_slots.T, source_group.T
    tile, width = feats.shape

    def over_nodes(step):
        pairs = [(n, along_ring(n, step, nodes)) for n in range(nodes)]
        return lax.ppermute(feats, "node", pairs)

    def over_chips(array, step):
        pairs = [(2 * z + c, 2 * along_ring(z, step, chips) + c) for z in range(chips) for c in range(2)]
        return lax.ppermute(array, "feat", pairs)

    def over_cores(array):
        return lax.ppermute(array, "feat", [(f, f ^ 1) for f in range(2 * chips)])

    rows_in = [over_nodes(step) for step in range(1, nodes)]
    adjacency, degree, chosen, own_feats, weight, bias = pl.pallas_call(
        prepare_kernel,
        out_shape=[
            jax.ShapeDtypeStruct((groups, tile, slots * tile), jnp.bfloat16),
            jax.ShapeDtypeStruct((groups, EXTRA, tile), jnp.float32),
            jax.ShapeDtypeStruct((groups * slots, 128), jnp.int32),
            jax.ShapeDtypeStruct(feats.shape, feats.dtype),
            jax.ShapeDtypeStruct(proj_weight.shape, proj_weight.dtype),
            jax.ShapeDtypeStruct((1, width), proj_bias.dtype),
        ],
        in_specs=[HBM] * 6,
        out_specs=[VMEM] * 6,
        scratch_shapes=[
            pltpu.SMEM(live_slots.shape, live_slots.dtype),
            pltpu.SMEM(source_group.shape, source_group.dtype),
            pltpu.VMEM(tile_values.shape, tile_values.dtype),
            pltpu.SemaphoreType.DMA((groups,)),
            pltpu.SemaphoreType.DMA((5,)),
        ],
        compiler_params=PARAMS,
        cost_estimate=pl.CostEstimate(flops=1 << 27, bytes_accessed=1 << 22, transcendentals=0),
    )(
        *(
            pltpu.with_memory_space_constraint(array, pltpu.HBM)
            for array in (live_slots, source_group, tile_values, feats, proj_weight, proj_bias.reshape(1, -1))
        )
    )
    rows_in = [own_feats] + rows_in

    def aggregate(mine, steps):
        dtype = jnp.float32
        return pl.pallas_call(
            functools.partial(aggregate_kernel, nodes, chips, slots, mine, steps),
            out_shape=jax.ShapeDtypeStruct((len(steps), tile + EXTRA, width), dtype),
            in_specs=[VMEM] * (3 + nodes),
            out_specs=VMEM,
            scratch_shapes=[pltpu.VMEM((nodes, tile, width), jnp.bfloat16)],
            compiler_params=PARAMS,
            cost_estimate=pl.CostEstimate(flops=1 << 27, bytes_accessed=1 << 22, transcendentals=0),
        )(chosen, adjacency, degree, *rows_in)

    def merge(mine, theirs, dtypes):
        return pl.pallas_call(
            merge_kernel,
            out_shape=[jax.ShapeDtypeStruct((tile + EXTRA, width), dtype) for dtype in dtypes],
            in_specs=[VMEM] * 2,
            out_specs=[VMEM] * len(dtypes),
            compiler_params=PARAMS,
        )(mine, theirs)

    cut = min(chips, FIRST + 1)
    far, near = list(range(1, cut)), list(range(cut, chips)) + [0]
    theirs_far = over_cores(aggregate(0, far))
    theirs_near = over_cores(aggregate(0, near))
    parts = merge(aggregate(1, far), theirs_far, [jnp.bfloat16] * len(far))
    *rest, own = merge(aggregate(1, near), theirs_near, [jnp.bfloat16] * (len(near) - 1) + [jnp.float32])
    parts = [over_chips(part, step) for step, part in enumerate([*parts, *rest], 1)]
    return pl.pallas_call(
        update_kernel,
        out_shape=jax.ShapeDtypeStruct((tile, width), jnp.bfloat16),
        in_specs=[VMEM] * (chips + 3),
        out_specs=VMEM,
        compiler_params=PARAMS,
    )(own, *parts, own_feats, weight, bias)


def solution(mesh):
    placed = (
        P(("node", "feat"), None),
        P("node", "feat", None, None),
        P("node", "feat"),
        P("node", "feat"),
        P(),
        P(),
    )
    return jax.shard_map(
        functools.partial(body, mesh),
        mesh=mesh,
        in_specs=placed,
        out_specs=P(("node", "feat"), None),
        check_vma=False,
    )
```

```python
import functools

import jax
import jax.numpy as jnp
from jax import lax
from jax.experimental import pallas as pl
from jax.experimental.pallas import tpu as pltpu
from jax.sharding import PartitionSpec as P

EXTRA = 8
FIRST = 2
VMEM = pl.BlockSpec(memory_space=pltpu.VMEM)
SMEM = pl.BlockSpec(memory_space=pltpu.SMEM)
HBM = pl.BlockSpec(memory_space=pltpu.HBM)
PARAMS = pltpu.CompilerParams(vmem_limit_bytes=32 * 1024 * 1024)


def along_ring(index, step, count):
    odd = index % 2
    place = odd * (count - 1) + (1 - 2 * odd) * (index // 2)
    place = (place + count - step) % count
    back = place // ((count + 1) // 2)
    return back * (2 * (count - 1 - place) + 1) + (1 - back) * 2 * place


def split_rows(degree):
    high = degree.astype(jnp.bfloat16)
    low = (degree - high.astype(jnp.float32)).astype(jnp.bfloat16)
    return jnp.concatenate([high, low], axis=1)


def join_rows(rows):
    rows = rows.astype(jnp.float32)
    half = rows.shape[1] // 2
    return rows[:, :half] + rows[:, half:]


def group_order(chips):
    chip, core = lax.axis_index("feat") // 2, lax.axis_index("feat") % 2
    return [
        along_ring(chip, step, chips) * 2 + (core if mine else 1 - core)
        for mine in range(2)
        for step in range(chips)
    ]


def prepare_kernel(
    live_in, src_in, tiles_in, feats_in, weight_in, bias_in,
    adjacency, degree, chosen, feats, weight, bias,
    live, src, tiles, tile_sems, sems,
):
    groups, slots, tile, _ = tiles.shape
    order = group_order(groups // 2)
    small = [
        pltpu.make_async_copy(live_in, live, sems.at[0]),
        pltpu.make_async_copy(src_in, src, sems.at[1]),
        pltpu.make_async_copy(feats_in, feats, sems.at[2]),
        pltpu.make_async_copy(weight_in, weight, sems.at[3]),
        pltpu.make_async_copy(bias_in, bias, sems.at[4]),
    ]
    large = [
        pltpu.make_async_copy(tiles_in.at[group], tiles.at[place], tile_sems.at[place])
        for place, group in enumerate(order)
    ]
    small[0].start()
    small[1].start()
    for copy in large:
        copy.start()
    for copy in small[2:]:
        copy.start()
    ones = jnp.ones((EXTRA, slots * tile), jnp.bfloat16)
    small[0].wait()
    small[1].wait()
    for place, group in enumerate(order):
        for slot in range(slots):
            row = place * slots + slot
            chosen[row : row + 1] = jnp.full((1, chosen.shape[1]), src[slot, group], jnp.int32)
    for place, group in enumerate(order):
        large[place].wait()
        count = live[0, group]
        wide = []
        for slot in range(slots):
            block = tiles[place, slot]
            wide.append(jnp.where(slot < count, block, jnp.zeros_like(block)))
        wide = jnp.concatenate(wide, axis=1)
        adjacency[place] = wide
        degree[place] = lax.dot_general(
            ones, wide, (((1,), (1,)), ((), ())), preferred_element_type=jnp.float32
        )
    for copy in small[2:]:
        copy.wait()


def aggregate_kernel(nodes, chips, slots, mine, steps, *refs):
    chosen, adjacency, degree = refs[:3]
    feats_in = refs[3 : 3 + nodes]
    out, rows = refs[-2:]
    node = lax.axis_index("node")
    tile = feats_in[0].shape[0]
    for step in range(nodes):
        rows[along_ring(node, (nodes - step) % nodes, nodes)] = feats_in[step][...]
    for index, step in enumerate(steps):
        place = mine * chips + step
        picks = [chosen[place * slots + slot, 0] for slot in range(slots)]
        right = jnp.concatenate([rows[pick] for pick in picks], axis=0)
        product = jnp.dot(adjacency[place], right, preferred_element_type=jnp.float32)
        out[index, :tile] = product.astype(out.dtype)
        out[index, tile:] = split_rows(degree[place]).astype(out.dtype)


def merge_kernel(first, count, mine, theirs, *outs):
    outs = outs[-count:]
    tile = mine.shape[1] - EXTRA
    for index, out in enumerate(outs):
        total = mine[first + index, :tile] + theirs[index, :tile].astype(jnp.float32)
        degree = split_rows(join_rows(mine[first + index, tile:]) + join_rows(theirs[index, tile:]))
        out[:tile] = total.astype(out.dtype)
        out[tile:] = degree.astype(out.dtype)


def gather_kernel(own, *refs):
    *parts, feats, out = refs
    tile = feats.shape[0]
    total = own[...]
    for part in parts:
        total = total + part[...].astype(jnp.float32)
    out[:tile] = total[:tile] + feats[...].astype(jnp.float32)
    out[tile:] = total[tile:]


def update_kernel(earlier, last, feats, weight, bias, out):
    tile = feats.shape[0]
    total = earlier[...] + last[...].astype(jnp.float32)
    degree = join_rows(total[tile:])[:1]
    scale = jnp.transpose(jnp.broadcast_to(lax.rsqrt(degree + 1.0), (tile, tile)))
    scale = jnp.concatenate([scale] * (feats.shape[1] // tile), axis=1)
    normed = (total[:tile] * scale).astype(jnp.bfloat16)
    hidden = jnp.dot(normed, weight[...], preferred_element_type=jnp.float32) + bias[...]
    out[...] = (feats[...].astype(jnp.float32) + jnp.maximum(hidden, 0.0)).astype(jnp.bfloat16)


def body(mesh, feats, tile_values, source_group, live_slots, proj_weight, proj_bias):
    nodes, chips = mesh.shape["node"], mesh.shape["feat"] // 2
    groups, slots = tile_values.shape[:2]
    live_slots, source_group = live_slots.T, source_group.T
    tile, width = feats.shape

    def over_nodes(step):
        pairs = [(n, along_ring(n, step, nodes)) for n in range(nodes)]
        return lax.ppermute(feats, "node", pairs)

    def over_chips(array, step):
        pairs = [(2 * z + c, 2 * along_ring(z, step, chips) + c) for z in range(chips) for c in range(2)]
        return lax.ppermute(array, "feat", pairs)

    def over_cores(array):
        return lax.ppermute(array, "feat", [(f, f ^ 1) for f in range(2 * chips)])

    rows_in = [over_nodes(step) for step in range(1, nodes)]
    adjacency, degree, chosen, own_feats, weight, bias = pl.pallas_call(
        prepare_kernel,
        out_shape=[
            jax.ShapeDtypeStruct((groups, tile, slots * tile), jnp.bfloat16),
            jax.ShapeDtypeStruct((groups, EXTRA, tile), jnp.float32),
            jax.ShapeDtypeStruct((groups * slots, 128), jnp.int32),
            jax.ShapeDtypeStruct(feats.shape, feats.dtype),
            jax.ShapeDtypeStruct(proj_weight.shape, proj_weight.dtype),
            jax.ShapeDtypeStruct((1, width), proj_bias.dtype),
        ],
        in_specs=[HBM] * 6,
        out_specs=[VMEM] * 6,
        scratch_shapes=[
            pltpu.SMEM(live_slots.shape, live_slots.dtype),
            pltpu.SMEM(source_group.shape, source_group.dtype),
            pltpu.VMEM(tile_values.shape, tile_values.dtype),
            pltpu.SemaphoreType.DMA((groups,)),
            pltpu.SemaphoreType.DMA((5,)),
        ],
        compiler_params=PARAMS,
        cost_estimate=pl.CostEstimate(flops=1 << 27, bytes_accessed=1 << 22, transcendentals=0),
    )(
        *(
            pltpu.with_memory_space_constraint(array, pltpu.HBM)
            for array in (live_slots, source_group, tile_values, feats, proj_weight, proj_bias.reshape(1, -1))
        )
    )
    rows_in = [own_feats] + rows_in

    def aggregate(mine, steps, *after):
        dtype = jnp.float32 if mine else jnp.bfloat16
        return pl.pallas_call(
            functools.partial(aggregate_kernel, nodes, chips, slots, mine, steps),
            out_shape=jax.ShapeDtypeStruct((len(steps), tile + EXTRA, width), dtype),
            in_specs=[VMEM] * (3 + nodes + len(after)),
            out_specs=VMEM,
            scratch_shapes=[pltpu.VMEM((nodes, tile, width), jnp.bfloat16)],
            compiler_params=PARAMS,
            cost_estimate=pl.CostEstimate(flops=1 << 27, bytes_accessed=1 << 22, transcendentals=0),
        )(chosen, adjacency, degree, *rows_in, *after)

    def merge(first, mine, theirs, dtypes, *after):
        return pl.pallas_call(
            functools.partial(merge_kernel, first, len(dtypes)),
            out_shape=[jax.ShapeDtypeStruct((tile + EXTRA, width), dtype) for dtype in dtypes],
            in_specs=[VMEM] * (2 + len(after)),
            out_specs=[VMEM] * len(dtypes),
            compiler_params=PARAMS,
        )(mine, theirs, *after)

    cut = min(chips, FIRST + 1)
    far, near = list(range(1, cut)), list(range(cut, chips)) + [0]
    first = aggregate(0, far)
    mine = aggregate(1, far + near, first)
    second = aggregate(0, near, mine)
    parts = merge(0, mine, over_cores(first), [jnp.bfloat16] * len(far))
    *rest, own = merge(
        len(far), mine, over_cores(second), [jnp.bfloat16] * (len(near) - 1) + [jnp.float32]
    )
    parts = [over_chips(part, step) for step, part in enumerate([*parts, *rest], 1)]
    *parts, last = parts
    earlier = pl.pallas_call(
        gather_kernel,
        out_shape=jax.ShapeDtypeStruct((tile + EXTRA, width), jnp.float32),
        in_specs=[VMEM] * (len(parts) + 2),
        out_specs=VMEM,
        compiler_params=PARAMS,
    )(own, *parts, own_feats)
    return pl.pallas_call(
        update_kernel,
        out_shape=jax.ShapeDtypeStruct((tile, width), jnp.bfloat16),
        in_specs=[VMEM] * 5,
        out_specs=VMEM,
        compiler_params=PARAMS,
    )(earlier, last, own_feats, weight, bias)


def solution(mesh):
    placed = (
        P(("node", "feat"), None),
        P("node", "feat", None, None),
        P("node", "feat"),
        P("node", "feat"),
        P(),
        P(),
    )
    return jax.shard_map(
        functools.partial(body, mesh),
        mesh=mesh,
        in_specs=placed,
        out_specs=P(("node", "feat"), None),
        check_vma=False,
    )
```

```python
import functools

import jax
import jax.numpy as jnp
from jax import lax
from jax.experimental import pallas as pl
from jax.experimental.pallas import tpu as pltpu
from jax.sharding import PartitionSpec as P

EXTRA = 8
FIRST = 2
VMEM = pl.BlockSpec(memory_space=pltpu.VMEM)
SMEM = pl.BlockSpec(memory_space=pltpu.SMEM)
HBM = pl.BlockSpec(memory_space=pltpu.HBM)
PARAMS = pltpu.CompilerParams(vmem_limit_bytes=32 * 1024 * 1024)


def along_ring(index, step, count):
    odd = index % 2
    place = odd * (count - 1) + (1 - 2 * odd) * (index // 2)
    place = (place + count - step) % count
    back = place // ((count + 1) // 2)
    return back * (2 * (count - 1 - place) + 1) + (1 - back) * 2 * place


def split_rows(degree):
    high = degree.astype(jnp.bfloat16)
    low = (degree - high.astype(jnp.float32)).astype(jnp.bfloat16)
    return jnp.concatenate([high, low], axis=1)


def join_rows(rows):
    rows = rows.astype(jnp.float32)
    half = rows.shape[1] // 2
    return rows[:, :half] + rows[:, half:]


def group_order(chips):
    chip, core = lax.axis_index("feat") // 2, lax.axis_index("feat") % 2
    return [
        along_ring(chip, step, chips) * 2 + (core if mine else 1 - core)
        for mine in range(2)
        for step in range(chips)
    ]


def prepare_kernel(
    live_in, src_in, tiles_in, feats_in, weight_in, bias_in,
    adjacency, degree, chosen, feats, weight, bias,
    live, src, tiles, tile_sems, sems,
):
    groups, slots, tile, _ = tiles.shape
    order = group_order(groups // 2)
    small = [
        pltpu.make_async_copy(live_in, live, sems.at[0]),
        pltpu.make_async_copy(src_in, src, sems.at[1]),
        pltpu.make_async_copy(feats_in, feats, sems.at[2]),
        pltpu.make_async_copy(weight_in, weight, sems.at[3]),
        pltpu.make_async_copy(bias_in, bias, sems.at[4]),
    ]
    large = [
        pltpu.make_async_copy(tiles_in.at[group], tiles.at[place], tile_sems.at[place])
        for place, group in enumerate(order)
    ]
    small[0].start()
    small[1].start()
    for copy in large:
        copy.start()
    for copy in small[2:]:
        copy.start()
    ones = jnp.ones((EXTRA, slots * tile), jnp.bfloat16)
    small[0].wait()
    small[1].wait()
    for place, group in enumerate(order):
        for slot in range(slots):
            row = place * slots + slot
            chosen[row : row + 1] = jnp.full((1, chosen.shape[1]), src[slot, group], jnp.int32)
    for place, group in enumerate(order):
        large[place].wait()
        count = live[0, group]
        wide = []
        for slot in range(slots):
            block = tiles[place, slot]
            wide.append(jnp.where(slot < count, block, jnp.zeros_like(block)))
        wide = jnp.concatenate(wide, axis=1)
        adjacency[place] = wide
        degree[place] = lax.dot_general(
            ones, wide, (((1,), (1,)), ((), ())), preferred_element_type=jnp.float32
        )
    for copy in small[2:]:
        copy.wait()


def aggregate_kernel(nodes, chips, slots, mine, steps, *refs):
    chosen, adjacency, degree = refs[:3]
    feats_in = refs[3 : 3 + nodes]
    out, rows = refs[-2:]
    node = lax.axis_index("node")
    tile = feats_in[0].shape[0]
    for step in range(nodes):
        rows[along_ring(node, (nodes - step) % nodes, nodes)] = feats_in[step][...]
    for index, step in enumerate(steps):
        place = mine * chips + step
        picks = [chosen[place * slots + slot, 0] for slot in range(slots)]
        right = jnp.concatenate([rows[pick] for pick in picks], axis=0)
        product = jnp.dot(adjacency[place], right, preferred_element_type=jnp.float32)
        out[index, :tile] = product.astype(out.dtype)
        out[index, tile:] = split_rows(degree[place]).astype(out.dtype)


def merge_kernel(first, count, mine, theirs, *outs):
    outs = outs[-count:]
    tile = mine.shape[1] - EXTRA
    for index, out in enumerate(outs):
        total = mine[first + index, :tile] + theirs[index, :tile].astype(jnp.float32)
        degree = split_rows(join_rows(mine[first + index, tile:]) + join_rows(theirs[index, tile:]))
        out[:tile] = total.astype(out.dtype)
        out[tile:] = degree.astype(out.dtype)


def gather_kernel(own, *refs):
    *parts, feats, out = refs
    tile = feats.shape[0]
    total = own[...]
    for part in parts:
        total = total + part[...].astype(jnp.float32)
    out[:tile] = total[:tile] + feats[...].astype(jnp.float32)
    out[tile:] = total[tile:]


def update_kernel(earlier, last, feats, weight, bias, out):
    tile = feats.shape[0]
    total = earlier[...] + last[...].astype(jnp.float32)
    degree = join_rows(total[tile:])[:1]
    scale = jnp.transpose(jnp.broadcast_to(lax.rsqrt(degree + 1.0), (tile, tile)))
    scale = jnp.concatenate([scale] * (feats.shape[1] // tile), axis=1)
    normed = (total[:tile] * scale).astype(jnp.bfloat16)
    hidden = jnp.dot(normed, weight[...], preferred_element_type=jnp.float32) + bias[...]
    out[...] = (feats[...].astype(jnp.float32) + jnp.maximum(hidden, 0.0)).astype(jnp.bfloat16)


def body(mesh, feats, tile_values, source_group, live_slots, proj_weight, proj_bias):
    nodes, chips = mesh.shape["node"], mesh.shape["feat"] // 2
    groups, slots = tile_values.shape[:2]
    live_slots, source_group = live_slots.T, source_group.T
    tile, width = feats.shape

    def over_nodes(step):
        pairs = [(n, along_ring(n, step, nodes)) for n in range(nodes)]
        return lax.ppermute(feats, "node", pairs)

    def over_chips(array, step):
        pairs = [(2 * z + c, 2 * along_ring(z, step, chips) + c) for z in range(chips) for c in range(2)]
        return lax.ppermute(array, "feat", pairs)

    def over_cores(array):
        return lax.ppermute(array, "feat", [(f, f ^ 1) for f in range(2 * chips)])

    rows_in = [over_nodes(step) for step in range(1, nodes)]
    adjacency, degree, chosen, own_feats, weight, bias = pl.pallas_call(
        prepare_kernel,
        out_shape=[
            jax.ShapeDtypeStruct((groups, tile, slots * tile), jnp.bfloat16),
            jax.ShapeDtypeStruct((groups, EXTRA, tile), jnp.float32),
            jax.ShapeDtypeStruct((groups * slots, 128), jnp.int32),
            jax.ShapeDtypeStruct(feats.shape, feats.dtype),
            jax.ShapeDtypeStruct(proj_weight.shape, proj_weight.dtype),
            jax.ShapeDtypeStruct((1, width), proj_bias.dtype),
        ],
        in_specs=[HBM] * 6,
        out_specs=[VMEM] * 6,
        scratch_shapes=[
            pltpu.SMEM(live_slots.shape, live_slots.dtype),
            pltpu.SMEM(source_group.shape, source_group.dtype),
            pltpu.VMEM(tile_values.shape, tile_values.dtype),
            pltpu.SemaphoreType.DMA((groups,)),
            pltpu.SemaphoreType.DMA((5,)),
        ],
        compiler_params=PARAMS,
        cost_estimate=pl.CostEstimate(flops=1 << 27, bytes_accessed=1 << 22, transcendentals=0),
    )(
        *(
            pltpu.with_memory_space_constraint(array, pltpu.HBM)
            for array in (live_slots, source_group, tile_values, feats, proj_weight, proj_bias.reshape(1, -1))
        )
    )
    rows_in = [own_feats] + rows_in

    def aggregate(mine, steps, *after):
        return pl.pallas_call(
            functools.partial(aggregate_kernel, nodes, chips, slots, mine, steps),
            out_shape=jax.ShapeDtypeStruct((len(steps), tile + EXTRA, width), jnp.float32),
            in_specs=[VMEM] * (3 + nodes + len(after)),
            out_specs=VMEM,
            scratch_shapes=[pltpu.VMEM((nodes, tile, width), jnp.bfloat16)],
            compiler_params=PARAMS,
            cost_estimate=pl.CostEstimate(flops=1 << 27, bytes_accessed=1 << 22, transcendentals=0),
        )(chosen, adjacency, degree, *rows_in, *after)

    def merge(first, mine, theirs, dtypes, *after):
        return pl.pallas_call(
            functools.partial(merge_kernel, first, len(dtypes)),
            out_shape=[jax.ShapeDtypeStruct((tile + EXTRA, width), dtype) for dtype in dtypes],
            in_specs=[VMEM] * (2 + len(after)),
            out_specs=[VMEM] * len(dtypes),
            compiler_params=PARAMS,
        )(mine, theirs, *after)

    cut = min(chips, FIRST + 1)
    far, near = list(range(1, cut)), list(range(cut, chips)) + [0]
    first = aggregate(0, far)
    mine = aggregate(1, far + near, first)
    second = aggregate(0, near, mine)
    parts = merge(0, mine, over_cores(first), [jnp.bfloat16] * len(far))
    *rest, own = merge(
        len(far), mine, over_cores(second), [jnp.bfloat16] * (len(near) - 1) + [jnp.float32]
    )
    parts = [over_chips(part, step) for step, part in enumerate([*parts, *rest], 1)]
    *parts, last = parts
    earlier = pl.pallas_call(
        gather_kernel,
        out_shape=jax.ShapeDtypeStruct((tile + EXTRA, width), jnp.float32),
        in_specs=[VMEM] * (len(parts) + 2),
        out_specs=VMEM,
        compiler_params=PARAMS,
    )(own, *parts, own_feats)
    return pl.pallas_call(
        update_kernel,
        out_shape=jax.ShapeDtypeStruct((tile, width), jnp.bfloat16),
        in_specs=[VMEM] * 5,
        out_specs=VMEM,
        compiler_params=PARAMS,
    )(earlier, last, own_feats, weight, bias)


def solution(mesh):
    placed = (
        P(("node", "feat"), None),
        P("node", "feat", None, None),
        P("node", "feat"),
        P("node", "feat"),
        P(),
        P(),
    )
    return jax.shard_map(
        functools.partial(body, mesh),
        mesh=mesh,
        in_specs=placed,
        out_specs=P(("node", "feat"), None),
        check_vma=False,
    )
```

```python
import functools

import jax
import jax.numpy as jnp
from jax import lax
from jax.experimental import pallas as pl
from jax.experimental.pallas import tpu as pltpu
from jax.sharding import PartitionSpec as P

EXTRA = 8
FIRST = 2
VMEM = pl.BlockSpec(memory_space=pltpu.VMEM)
SMEM = pl.BlockSpec(memory_space=pltpu.SMEM)
HBM = pl.BlockSpec(memory_space=pltpu.HBM)
PARAMS = pltpu.CompilerParams(vmem_limit_bytes=32 * 1024 * 1024)


def along_ring(index, step, count):
    odd = index % 2
    place = odd * (count - 1) + (1 - 2 * odd) * (index // 2)
    place = (place + count - step) % count
    back = place // ((count + 1) // 2)
    return back * (2 * (count - 1 - place) + 1) + (1 - back) * 2 * place


def split_rows(degree):
    high = degree.astype(jnp.bfloat16)
    low = (degree - high.astype(jnp.float32)).astype(jnp.bfloat16)
    return jnp.concatenate([high, low], axis=1)


def join_rows(rows):
    rows = rows.astype(jnp.float32)
    half = rows.shape[1] // 2
    return rows[:, :half] + rows[:, half:]


def group_order(chips):
    chip, core = lax.axis_index("feat") // 2, lax.axis_index("feat") % 2
    return [
        along_ring(chip, step, chips) * 2 + (core if mine else 1 - core)
        for mine in range(2)
        for step in range(chips)
    ]


def prepare_kernel(
    live_in, src_in, tiles_in, feats_in, weight_in, bias_in,
    adjacency, degree, chosen, feats, weight, bias,
    live, src, tiles, tile_sems, sems,
):
    groups, slots, tile, _ = tiles.shape
    order = group_order(groups // 2)
    small = [
        pltpu.make_async_copy(live_in, live, sems.at[0]),
        pltpu.make_async_copy(src_in, src, sems.at[1]),
        pltpu.make_async_copy(feats_in, feats, sems.at[2]),
        pltpu.make_async_copy(weight_in, weight, sems.at[3]),
        pltpu.make_async_copy(bias_in, bias, sems.at[4]),
    ]
    large = [
        pltpu.make_async_copy(tiles_in.at[group], tiles.at[place], tile_sems.at[place])
        for place, group in enumerate(order)
    ]
    small[0].start()
    small[1].start()
    for copy in large:
        copy.start()
    for copy in small[2:]:
        copy.start()
    ones = jnp.ones((EXTRA, slots * tile), jnp.bfloat16)
    small[0].wait()
    small[1].wait()
    for place, group in enumerate(order):
        for slot in range(slots):
            row = place * slots + slot
            chosen[row : row + 1] = jnp.full((1, chosen.shape[1]), src[slot, group], jnp.int32)
    for place, group in enumerate(order):
        large[place].wait()
        count = live[0, group]
        wide = []
        for slot in range(slots):
            block = tiles[place, slot]
            wide.append(jnp.where(slot < count, block, jnp.zeros_like(block)))
        wide = jnp.concatenate(wide, axis=1)
        adjacency[place] = wide
        degree[place] = lax.dot_general(
            ones, wide, (((1,), (1,)), ((), ())), preferred_element_type=jnp.float32
        )
    for copy in small[2:]:
        copy.wait()


def stack_kernel(steps, nodes, *refs):
    *feats_in, rows = refs
    node = lax.axis_index("node")
    for feats, step in zip(feats_in, steps):
        rows[along_ring(node, (nodes - step) % nodes, nodes)] = feats[...]


def aggregate_kernel(nodes, chips, slots, mine, steps, late, *refs):
    chosen, adjacency, degree, rows = refs[:4]
    out = refs[-1]
    if late is not None:
        out, rows = refs[-2:]
        rows[along_ring(lax.axis_index("node"), (nodes - late) % nodes, nodes)] = refs[4][...]
    tile = rows.shape[1]
    for index, step in enumerate(steps):
        place = mine * chips + step
        picks = [chosen[place * slots + slot, 0] for slot in range(slots)]
        right = jnp.concatenate([rows[pick] for pick in picks], axis=0)
        product = jnp.dot(adjacency[place], right, preferred_element_type=jnp.float32)
        out[index, :tile] = product.astype(out.dtype)
        out[index, tile:] = split_rows(degree[place]).astype(out.dtype)


def merge_kernel(first, count, mine, theirs, *outs):
    outs = outs[-count:]
    tile = mine.shape[1] - EXTRA
    for index, out in enumerate(outs):
        total = mine[first + index, :tile] + theirs[index, :tile].astype(jnp.float32)
        degree = split_rows(join_rows(mine[first + index, tile:]) + join_rows(theirs[index, tile:]))
        out[:tile] = total.astype(out.dtype)
        out[tile:] = degree.astype(out.dtype)


def gather_kernel(own, *refs):
    *parts, feats, out = refs
    tile = feats.shape[0]
    total = own[...]
    for part in parts:
        total = total + part[...].astype(jnp.float32)
    out[:tile] = total[:tile] + feats[...].astype(jnp.float32)
    out[tile:] = total[tile:]


def update_kernel(earlier, last, feats, weight, bias, out):
    tile = feats.shape[0]
    total = earlier[...] + last[...].astype(jnp.float32)
    degree = join_rows(total[tile:])[:1]
    scale = jnp.transpose(jnp.broadcast_to(lax.rsqrt(degree + 1.0), (tile, tile)))
    scale = jnp.concatenate([scale] * (feats.shape[1] // tile), axis=1)
    normed = (total[:tile] * scale).astype(jnp.bfloat16)
    hidden = jnp.dot(normed, weight[...], preferred_element_type=jnp.float32) + bias[...]
    out[...] = (feats[...].astype(jnp.float32) + jnp.maximum(hidden, 0.0)).astype(jnp.bfloat16)


def body(mesh, feats, tile_values, source_group, live_slots, proj_weight, proj_bias):
    nodes, chips = mesh.shape["node"], mesh.shape["feat"] // 2
    groups, slots = tile_values.shape[:2]
    live_slots, source_group = live_slots.T, source_group.T
    tile, width = feats.shape

    def over_nodes(step):
        pairs = [(n, along_ring(n, step, nodes)) for n in range(nodes)]
        return lax.ppermute(feats, "node", pairs)

    def over_chips(array, step):
        pairs = [(2 * z + c, 2 * along_ring(z, step, chips) + c) for z in range(chips) for c in range(2)]
        return lax.ppermute(array, "feat", pairs)

    def over_cores(array):
        return lax.ppermute(array, "feat", [(f, f ^ 1) for f in range(2 * chips)])

    rows_in = [over_nodes(step) for step in range(1, nodes)]
    adjacency, degree, chosen, own_feats, weight, bias = pl.pallas_call(
        prepare_kernel,
        out_shape=[
            jax.ShapeDtypeStruct((groups, tile, slots * tile), jnp.bfloat16),
            jax.ShapeDtypeStruct((groups, EXTRA, tile), jnp.float32),
            jax.ShapeDtypeStruct((groups * slots, 128), jnp.int32),
            jax.ShapeDtypeStruct(feats.shape, feats.dtype),
            jax.ShapeDtypeStruct(proj_weight.shape, proj_weight.dtype),
            jax.ShapeDtypeStruct((1, width), proj_bias.dtype),
        ],
        in_specs=[HBM] * 6,
        out_specs=[VMEM] * 6,
        scratch_shapes=[
            pltpu.SMEM(live_slots.shape, live_slots.dtype),
            pltpu.SMEM(source_group.shape, source_group.dtype),
            pltpu.VMEM(tile_values.shape, tile_values.dtype),
            pltpu.SemaphoreType.DMA((groups,)),
            pltpu.SemaphoreType.DMA((5,)),
        ],
        compiler_params=PARAMS,
        cost_estimate=pl.CostEstimate(flops=1 << 27, bytes_accessed=1 << 22, transcendentals=0),
    )(
        *(
            pltpu.with_memory_space_constraint(array, pltpu.HBM)
            for array in (live_slots, source_group, tile_values, feats, proj_weight, proj_bias.reshape(1, -1))
        )
    )
    rows_in = [own_feats] + rows_in

    late = nodes // 2
    early = [step for step in range(nodes) if step != late]
    stack = jax.ShapeDtypeStruct((nodes, tile, width), jnp.bfloat16)
    rows = pl.pallas_call(
        functools.partial(stack_kernel, early, nodes),
        out_shape=stack,
        in_specs=[VMEM] * len(early),
        out_specs=VMEM,
        compiler_params=PARAMS,
    )(*(rows_in[step] for step in early))

    def aggregate(mine, steps, rows, *more, late=None):
        dtype = jnp.float32 if mine else jnp.bfloat16
        out = jax.ShapeDtypeStruct((len(steps), tile + EXTRA, width), dtype)
        first = late is not None
        return pl.pallas_call(
            functools.partial(aggregate_kernel, nodes, chips, slots, mine, steps, late),
            out_shape=[out, stack] if first else out,
            in_specs=[VMEM] * (4 + len(more)),
            out_specs=[VMEM] * 2 if first else VMEM,
            input_output_aliases={3: 1} if first else {},
            compiler_params=PARAMS,
            cost_estimate=pl.CostEstimate(flops=1 << 27, bytes_accessed=1 << 22, transcendentals=0),
        )(chosen, adjacency, degree, rows, *more)

    def merge(first, mine, theirs, dtypes, *after):
        return pl.pallas_call(
            functools.partial(merge_kernel, first, len(dtypes)),
            out_shape=[jax.ShapeDtypeStruct((tile + EXTRA, width), dtype) for dtype in dtypes],
            in_specs=[VMEM] * (2 + len(after)),
            out_specs=[VMEM] * len(dtypes),
            compiler_params=PARAMS,
        )(mine, theirs, *after)

    cut = min(chips, FIRST + 1)
    far, near = list(range(1, cut)), list(range(cut, chips)) + [0]
    first, rows = aggregate(0, far, rows, rows_in[late], late=late)
    mine = aggregate(1, far + near, rows, first)
    second = aggregate(0, near, rows, mine)
    parts = merge(0, mine, over_cores(first), [jnp.bfloat16] * len(far))
    *rest, own = merge(
        len(far), mine, over_cores(second), [jnp.bfloat16] * (len(near) - 1) + [jnp.float32]
    )
    parts = [over_chips(part, step) for step, part in enumerate([*parts, *rest], 1)]
    *parts, last = parts
    earlier = pl.pallas_call(
        gather_kernel,
        out_shape=jax.ShapeDtypeStruct((tile + EXTRA, width), jnp.float32),
        in_specs=[VMEM] * (len(parts) + 2),
        out_specs=VMEM,
        compiler_params=PARAMS,
    )(own, *parts, own_feats)
    return pl.pallas_call(
        update_kernel,
        out_shape=jax.ShapeDtypeStruct((tile, width), jnp.bfloat16),
        in_specs=[VMEM] * 5,
        out_specs=VMEM,
        compiler_params=PARAMS,
    )(earlier, last, own_feats, weight, bias)


def solution(mesh):
    placed = (
        P(("node", "feat"), None),
        P("node", "feat", None, None),
        P("node", "feat"),
        P("node", "feat"),
        P(),
        P(),
    )
    return jax.shard_map(
        functools.partial(body, mesh),
        mesh=mesh,
        in_specs=placed,
        out_specs=P(("node", "feat"), None),
        check_vma=False,
    )
```

```python
import functools

import jax
import jax.numpy as jnp
from jax import lax
from jax.experimental import pallas as pl
from jax.experimental.pallas import tpu as pltpu
from jax.sharding import PartitionSpec as P

EXTRA = 8
FIRST = 2
VMEM = pl.BlockSpec(memory_space=pltpu.VMEM)
SMEM = pl.BlockSpec(memory_space=pltpu.SMEM)
HBM = pl.BlockSpec(memory_space=pltpu.HBM)
PARAMS = pltpu.CompilerParams(vmem_limit_bytes=32 * 1024 * 1024)


def along_ring(index, step, count):
    odd = index % 2
    place = odd * (count - 1) + (1 - 2 * odd) * (index // 2)
    place = (place + count - step) % count
    back = place // ((count + 1) // 2)
    return back * (2 * (count - 1 - place) + 1) + (1 - back) * 2 * place


def split_rows(degree):
    high = degree.astype(jnp.bfloat16)
    low = (degree - high.astype(jnp.float32)).astype(jnp.bfloat16)
    return jnp.concatenate([high, low], axis=1)


def join_rows(rows):
    rows = rows.astype(jnp.float32)
    half = rows.shape[1] // 2
    return rows[:, :half] + rows[:, half:]


def group_order(chips):
    chip, core = lax.axis_index("feat") // 2, lax.axis_index("feat") % 2
    return [
        along_ring(chip, step, chips) * 2 + (core if mine else 1 - core)
        for mine in range(2)
        for step in range(chips)
    ]


def prepare_kernel(
    live_in, src_in, tiles_in, feats_in, weight_in, bias_in,
    adjacency, degree, chosen, feats, weight, bias,
    live, src, tiles, tile_sems, sems,
):
    groups, slots, tile, _ = tiles.shape
    order = group_order(groups // 2)
    small = [
        pltpu.make_async_copy(live_in, live, sems.at[0]),
        pltpu.make_async_copy(src_in, src, sems.at[1]),
        pltpu.make_async_copy(feats_in, feats, sems.at[2]),
        pltpu.make_async_copy(weight_in, weight, sems.at[3]),
        pltpu.make_async_copy(bias_in, bias, sems.at[4]),
    ]
    large = [
        pltpu.make_async_copy(tiles_in.at[group], tiles.at[place], tile_sems.at[place])
        for place, group in enumerate(order)
    ]
    small[0].start()
    small[1].start()
    for copy in large:
        copy.start()
    for copy in small[2:]:
        copy.start()
    ones = jnp.ones((EXTRA, slots * tile), jnp.bfloat16)
    small[0].wait()
    small[1].wait()
    for place, group in enumerate(order):
        for slot in range(slots):
            row = place * slots + slot
            chosen[row : row + 1] = jnp.full((1, chosen.shape[1]), src[slot, group], jnp.int32)
    for place, group in enumerate(order):
        large[place].wait()
        count = live[0, group]
        wide = []
        for slot in range(slots):
            block = tiles[place, slot]
            wide.append(jnp.where(slot < count, block, jnp.zeros_like(block)))
        wide = jnp.concatenate(wide, axis=1)
        adjacency[place] = wide
        degree[place] = lax.dot_general(
            ones, wide, (((1,), (1,)), ((), ())), preferred_element_type=jnp.float32
        )
    for copy in small[2:]:
        copy.wait()


def stack_kernel(steps, nodes, *refs):
    *feats_in, rows = refs
    node = lax.axis_index("node")
    for feats, step in zip(feats_in, steps):
        rows[along_ring(node, (nodes - step) % nodes, nodes)] = feats[...]


def aggregate_kernel(nodes, chips, slots, mine, steps, late, *refs):
    chosen, adjacency, degree, rows = refs[:4]
    out = refs[-1]
    if late is not None:
        out, rows = refs[-2:]
        rows[along_ring(lax.axis_index("node"), (nodes - late) % nodes, nodes)] = refs[4][...]
    tile = rows.shape[1]
    for index, step in enumerate(steps):
        place = mine * chips + step
        picks = [chosen[place * slots + slot, 0] for slot in range(slots)]
        right = jnp.concatenate([rows[pick] for pick in picks], axis=0)
        product = jnp.dot(adjacency[place], right, preferred_element_type=jnp.float32)
        out[index, :tile] = product.astype(out.dtype)
        out[index, tile:] = split_rows(degree[place]).astype(out.dtype)


def merge_kernel(first, count, mine, theirs, *outs):
    outs = outs[-count:]
    tile = mine.shape[1] - EXTRA
    for index, out in enumerate(outs):
        total = mine[first + index, :tile] + theirs[index, :tile].astype(jnp.float32)
        degree = split_rows(join_rows(mine[first + index, tile:]) + join_rows(theirs[index, tile:]))
        out[:tile] = total.astype(out.dtype)
        out[tile:] = degree.astype(out.dtype)


def gather_kernel(own, *refs):
    *parts, feats, out = refs
    tile = feats.shape[0]
    total = own[...]
    for part in parts:
        total = total + part[...].astype(jnp.float32)
    out[:tile] = total[:tile] + feats[...].astype(jnp.float32)
    out[tile:] = total[tile:]


def update_kernel(earlier, last, feats, weight, bias, out):
    tile = feats.shape[0]
    total = earlier[...] + last[...].astype(jnp.float32)
    degree = join_rows(total[tile:])[:1]
    scale = jnp.transpose(jnp.broadcast_to(lax.rsqrt(degree + 1.0), (tile, tile)))
    scale = jnp.concatenate([scale] * (feats.shape[1] // tile), axis=1)
    normed = (total[:tile] * scale).astype(jnp.bfloat16)
    hidden = jnp.dot(normed, weight[...], preferred_element_type=jnp.float32) + bias[...]
    out[...] = (feats[...].astype(jnp.float32) + jnp.maximum(hidden, 0.0)).astype(jnp.bfloat16)


def body(mesh, feats, tile_values, source_group, live_slots, proj_weight, proj_bias):
    nodes, chips = mesh.shape["node"], mesh.shape["feat"] // 2
    groups, slots = tile_values.shape[:2]
    live_slots, source_group = live_slots.T, source_group.T
    tile, width = feats.shape

    def over_nodes(step):
        pairs = [(n, along_ring(n, step, nodes)) for n in range(nodes)]
        return lax.ppermute(feats, "node", pairs)

    def over_chips(array, step):
        pairs = [(2 * z + c, 2 * along_ring(z, step, chips) + c) for z in range(chips) for c in range(2)]
        return lax.ppermute(array, "feat", pairs)

    def over_cores(array):
        return lax.ppermute(array, "feat", [(f, f ^ 1) for f in range(2 * chips)])

    rows_in = [over_nodes(step) for step in range(1, nodes)]
    adjacency, degree, chosen, own_feats, weight, bias = pl.pallas_call(
        prepare_kernel,
        out_shape=[
            jax.ShapeDtypeStruct((groups, tile, slots * tile), jnp.bfloat16),
            jax.ShapeDtypeStruct((groups, EXTRA, tile), jnp.float32),
            jax.ShapeDtypeStruct((groups * slots, 128), jnp.int32),
            jax.ShapeDtypeStruct(feats.shape, feats.dtype),
            jax.ShapeDtypeStruct(proj_weight.shape, proj_weight.dtype),
            jax.ShapeDtypeStruct((1, width), proj_bias.dtype),
        ],
        in_specs=[HBM] * 6,
        out_specs=[VMEM] * 6,
        scratch_shapes=[
            pltpu.SMEM(live_slots.shape, live_slots.dtype),
            pltpu.SMEM(source_group.shape, source_group.dtype),
            pltpu.VMEM(tile_values.shape, tile_values.dtype),
            pltpu.SemaphoreType.DMA((groups,)),
            pltpu.SemaphoreType.DMA((5,)),
        ],
        compiler_params=PARAMS,
        cost_estimate=pl.CostEstimate(flops=1 << 27, bytes_accessed=1 << 22, transcendentals=0),
    )(
        *(
            pltpu.with_memory_space_constraint(array, pltpu.HBM)
            for array in (live_slots, source_group, tile_values, feats, proj_weight, proj_bias.reshape(1, -1))
        )
    )
    rows_in = [own_feats] + rows_in

    late = 1
    early = [step for step in range(nodes) if step != late]
    stack = jax.ShapeDtypeStruct((nodes, tile, width), jnp.bfloat16)
    rows = pl.pallas_call(
        functools.partial(stack_kernel, early, nodes),
        out_shape=stack,
        in_specs=[VMEM] * len(early),
        out_specs=VMEM,
        compiler_params=PARAMS,
    )(*(rows_in[step] for step in early))

    def aggregate(mine, steps, rows, *more, late=None):
        dtype = jnp.float32 if mine else jnp.bfloat16
        out = jax.ShapeDtypeStruct((len(steps), tile + EXTRA, width), dtype)
        first = late is not None
        return pl.pallas_call(
            functools.partial(aggregate_kernel, nodes, chips, slots, mine, steps, late),
            out_shape=[out, stack] if first else out,
            in_specs=[VMEM] * (4 + len(more)),
            out_specs=[VMEM] * 2 if first else VMEM,
            input_output_aliases={3: 1} if first else {},
            compiler_params=PARAMS,
            cost_estimate=pl.CostEstimate(flops=1 << 27, bytes_accessed=1 << 22, transcendentals=0),
        )(chosen, adjacency, degree, rows, *more)

    def merge(first, mine, theirs, dtypes, *after):
        return pl.pallas_call(
            functools.partial(merge_kernel, first, len(dtypes)),
            out_shape=[jax.ShapeDtypeStruct((tile + EXTRA, width), dtype) for dtype in dtypes],
            in_specs=[VMEM] * (2 + len(after)),
            out_specs=[VMEM] * len(dtypes),
            compiler_params=PARAMS,
        )(mine, theirs, *after)

    cut = min(chips, FIRST + 1)
    far, near = list(range(1, cut)), list(range(cut, chips)) + [0]
    first, rows = aggregate(0, far, rows, rows_in[late], late=late)
    mine = aggregate(1, far + near, rows, first)
    second = aggregate(0, near, rows, mine)
    parts = merge(0, mine, over_cores(first), [jnp.bfloat16] * len(far))
    *rest, own = merge(
        len(far), mine, over_cores(second), [jnp.bfloat16] * (len(near) - 1) + [jnp.float32]
    )
    parts = [over_chips(part, step) for step, part in enumerate([*parts, *rest], 1)]
    *parts, last = parts
    earlier = pl.pallas_call(
        gather_kernel,
        out_shape=jax.ShapeDtypeStruct((tile + EXTRA, width), jnp.float32),
        in_specs=[VMEM] * (len(parts) + 2),
        out_specs=VMEM,
        compiler_params=PARAMS,
    )(own, *parts, own_feats)
    return pl.pallas_call(
        update_kernel,
        out_shape=jax.ShapeDtypeStruct((tile, width), jnp.bfloat16),
        in_specs=[VMEM] * 5,
        out_specs=VMEM,
        compiler_params=PARAMS,
    )(earlier, last, own_feats, weight, bias)


def solution(mesh):
    placed = (
        P(("node", "feat"), None),
        P("node", "feat", None, None),
        P("node", "feat"),
        P("node", "feat"),
        P(),
        P(),
    )
    return jax.shard_map(
        functools.partial(body, mesh),
        mesh=mesh,
        in_specs=placed,
        out_specs=P(("node", "feat"), None),
        check_vma=False,
    )
```

```python
import functools

import jax
import jax.numpy as jnp
from jax import lax
from jax.experimental import pallas as pl
from jax.experimental.pallas import tpu as pltpu
from jax.sharding import PartitionSpec as P

EXTRA = 8
FIRST = 2
VMEM = pl.BlockSpec(memory_space=pltpu.VMEM)
SMEM = pl.BlockSpec(memory_space=pltpu.SMEM)
HBM = pl.BlockSpec(memory_space=pltpu.HBM)
PARAMS = pltpu.CompilerParams(vmem_limit_bytes=32 * 1024 * 1024)


def along_ring(index, step, count):
    odd = index % 2
    place = odd * (count - 1) + (1 - 2 * odd) * (index // 2)
    place = (place + count - step) % count
    back = place // ((count + 1) // 2)
    return back * (2 * (count - 1 - place) + 1) + (1 - back) * 2 * place


def split_rows(degree):
    high = degree.astype(jnp.bfloat16)
    low = (degree - high.astype(jnp.float32)).astype(jnp.bfloat16)
    return jnp.concatenate([high, low], axis=1)


def join_rows(rows):
    rows = rows.astype(jnp.float32)
    half = rows.shape[1] // 2
    return rows[:, :half] + rows[:, half:]


def group_order(chips):
    chip, core = lax.axis_index("feat") // 2, lax.axis_index("feat") % 2
    return [
        along_ring(chip, step, chips) * 2 + (core if mine else 1 - core)
        for mine in range(2)
        for step in range(chips)
    ]


def prepare_kernel(
    live_in, src_in, tiles_in, feats_in, weight_in, bias_in,
    adjacency, degree, chosen, feats, weight, bias,
    live, src, tiles, tile_sems, sems,
):
    groups, slots, tile, _ = tiles.shape
    order = group_order(groups // 2)
    small = [
        pltpu.make_async_copy(live_in, live, sems.at[0]),
        pltpu.make_async_copy(src_in, src, sems.at[1]),
        pltpu.make_async_copy(feats_in, feats, sems.at[2]),
        pltpu.make_async_copy(weight_in, weight, sems.at[3]),
        pltpu.make_async_copy(bias_in, bias, sems.at[4]),
    ]
    large = [
        pltpu.make_async_copy(tiles_in.at[group], tiles.at[place], tile_sems.at[place])
        for place, group in enumerate(order)
    ]
    small[0].start()
    small[1].start()
    for copy in large:
        copy.start()
    for copy in small[2:]:
        copy.start()
    ones = jnp.ones((EXTRA, slots * tile), jnp.bfloat16)
    small[0].wait()
    small[1].wait()
    for place, group in enumerate(order):
        for slot in range(slots):
            row = place * slots + slot
            chosen[row : row + 1] = jnp.full((1, chosen.shape[1]), src[slot, group], jnp.int32)
    for place, group in enumerate(order):
        large[place].wait()
        count = live[0, group]
        wide = []
        for slot in range(slots):
            block = tiles[place, slot]
            wide.append(jnp.where(slot < count, block, jnp.zeros_like(block)))
        wide = jnp.concatenate(wide, axis=1)
        adjacency[place] = wide
        degree[place] = lax.dot_general(
            ones, wide, (((1,), (1,)), ((), ())), preferred_element_type=jnp.float32
        )
    for copy in small[2:]:
        copy.wait()


def aggregate_kernel(nodes, chips, slots, mine, steps, *refs):
    chosen, adjacency, degree = refs[:3]
    feats_in = refs[3 : 3 + nodes]
    out, rows = refs[-2:]
    node = lax.axis_index("node")
    tile = feats_in[0].shape[0]
    for step in range(nodes):
        rows[along_ring(node, (nodes - step) % nodes, nodes)] = feats_in[step][...]
    for index, step in enumerate(steps):
        place = mine * chips + step
        picks = [chosen[place * slots + slot, 0] for slot in range(slots)]
        right = jnp.concatenate([rows[pick] for pick in picks], axis=0)
        product = jnp.dot(adjacency[place], right, preferred_element_type=jnp.float32)
        out[index, :tile] = product.astype(out.dtype)
        out[index, tile:] = split_rows(degree[place]).astype(out.dtype)


def merge_kernel(first, skip, count, mine, theirs, *outs):
    outs = outs[-count:]
    tile = mine.shape[1] - EXTRA
    for index, out in enumerate(outs):
        total = mine[first + index, :tile] + theirs[skip + index, :tile].astype(jnp.float32)
        degree = split_rows(join_rows(mine[first + index, tile:]) + join_rows(theirs[skip + index, tile:]))
        out[:tile] = total.astype(out.dtype)
        out[tile:] = degree.astype(out.dtype)


def gather_kernel(own, *refs):
    *parts, feats, out = refs
    tile = feats.shape[0]
    total = own[...]
    for part in parts:
        total = total + part[...].astype(jnp.float32)
    out[:tile] = total[:tile] + feats[...].astype(jnp.float32)
    out[tile:] = total[tile:]


def update_kernel(earlier, last, feats, weight, bias, out):
    tile = feats.shape[0]
    total = earlier[...] + last[...].astype(jnp.float32)
    degree = join_rows(total[tile:])[:1]
    scale = jnp.transpose(jnp.broadcast_to(lax.rsqrt(degree + 1.0), (tile, tile)))
    scale = jnp.concatenate([scale] * (feats.shape[1] // tile), axis=1)
    normed = (total[:tile] * scale).astype(jnp.bfloat16)
    hidden = jnp.dot(normed, weight[...], preferred_element_type=jnp.float32) + bias[...]
    out[...] = (feats[...].astype(jnp.float32) + jnp.maximum(hidden, 0.0)).astype(jnp.bfloat16)


def body(mesh, feats, tile_values, source_group, live_slots, proj_weight, proj_bias):
    nodes, chips = mesh.shape["node"], mesh.shape["feat"] // 2
    groups, slots = tile_values.shape[:2]
    live_slots, source_group = live_slots.T, source_group.T
    tile, width = feats.shape

    def over_nodes(step):
        pairs = [(n, along_ring(n, step, nodes)) for n in range(nodes)]
        return lax.ppermute(feats, "node", pairs)

    def over_chips(array, step):
        pairs = [(2 * z + c, 2 * along_ring(z, step, chips) + c) for z in range(chips) for c in range(2)]
        return lax.ppermute(array, "feat", pairs)

    def over_cores(array):
        return lax.ppermute(array, "feat", [(f, f ^ 1) for f in range(2 * chips)])

    rows_in = [over_nodes(step) for step in range(1, nodes)]
    adjacency, degree, chosen, own_feats, weight, bias = pl.pallas_call(
        prepare_kernel,
        out_shape=[
            jax.ShapeDtypeStruct((groups, tile, slots * tile), jnp.bfloat16),
            jax.ShapeDtypeStruct((groups, EXTRA, tile), jnp.float32),
            jax.ShapeDtypeStruct((groups * slots, 128), jnp.int32),
            jax.ShapeDtypeStruct(feats.shape, feats.dtype),
            jax.ShapeDtypeStruct(proj_weight.shape, proj_weight.dtype),
            jax.ShapeDtypeStruct((1, width), proj_bias.dtype),
        ],
        in_specs=[HBM] * 6,
        out_specs=[VMEM] * 6,
        scratch_shapes=[
            pltpu.SMEM(live_slots.shape, live_slots.dtype),
            pltpu.SMEM(source_group.shape, source_group.dtype),
            pltpu.VMEM(tile_values.shape, tile_values.dtype),
            pltpu.SemaphoreType.DMA((groups,)),
            pltpu.SemaphoreType.DMA((5,)),
        ],
        compiler_params=PARAMS,
        cost_estimate=pl.CostEstimate(flops=1 << 27, bytes_accessed=1 << 22, transcendentals=0),
    )(
        *(
            pltpu.with_memory_space_constraint(array, pltpu.HBM)
            for array in (live_slots, source_group, tile_values, feats, proj_weight, proj_bias.reshape(1, -1))
        )
    )
    rows_in = [own_feats] + rows_in

    def aggregate(mine, steps, *after):
        dtype = jnp.float32 if mine else jnp.bfloat16
        return pl.pallas_call(
            functools.partial(aggregate_kernel, nodes, chips, slots, mine, steps),
            out_shape=jax.ShapeDtypeStruct((len(steps), tile + EXTRA, width), dtype),
            in_specs=[VMEM] * (3 + nodes + len(after)),
            out_specs=VMEM,
            scratch_shapes=[pltpu.VMEM((nodes, tile, width), jnp.bfloat16)],
            compiler_params=PARAMS,
            cost_estimate=pl.CostEstimate(flops=1 << 27, bytes_accessed=1 << 22, transcendentals=0),
        )(chosen, adjacency, degree, *rows_in, *after)

    def merge(first, skip, mine, theirs, dtypes, *after):
        return pl.pallas_call(
            functools.partial(merge_kernel, first, skip, len(dtypes)),
            out_shape=[jax.ShapeDtypeStruct((tile + EXTRA, width), dtype) for dtype in dtypes],
            in_specs=[VMEM] * (2 + len(after)),
            out_specs=[VMEM] * len(dtypes),
            compiler_params=PARAMS,
        )(mine, theirs, *after)

    cut = min(chips, FIRST + 1)
    far, near = list(range(1, cut)), list(range(cut, chips)) + [0]
    first = aggregate(0, far)
    mine = aggregate(1, far + near, first)
    second = aggregate(0, near, mine)
    swapped, parts = over_cores(first), []
    for index in range(len(far)):
        parts += merge(index, index, mine, swapped, [jnp.bfloat16], *parts[-1:])
    *rest, own = merge(
        len(far), 0, mine, over_cores(second), [jnp.bfloat16] * (len(near) - 1) + [jnp.float32]
    )
    parts = [over_chips(part, step) for step, part in enumerate([*parts, *rest], 1)]
    *parts, last = parts
    earlier = pl.pallas_call(
        gather_kernel,
        out_shape=jax.ShapeDtypeStruct((tile + EXTRA, width), jnp.float32),
        in_specs=[VMEM] * (len(parts) + 2),
        out_specs=VMEM,
        compiler_params=PARAMS,
    )(own, *parts, own_feats)
    return pl.pallas_call(
        update_kernel,
        out_shape=jax.ShapeDtypeStruct((tile, width), jnp.bfloat16),
        in_specs=[VMEM] * 5,
        out_specs=VMEM,
        compiler_params=PARAMS,
    )(earlier, last, own_feats, weight, bias)


def solution(mesh):
    placed = (
        P(("node", "feat"), None),
        P("node", "feat", None, None),
        P("node", "feat"),
        P("node", "feat"),
        P(),
        P(),
    )
    return jax.shard_map(
        functools.partial(body, mesh),
        mesh=mesh,
        in_specs=placed,
        out_specs=P(("node", "feat"), None),
        check_vma=False,
    )
```
